32 devices in a mesh: groups: 2 (over y), feat: 8 (over z, core), tok: 2 (over x).
Axes of the slice: x: 2, y: 2, z: 4, core: 2. Of those that a mesh axis runs over, the one named last changes fastest.
Arguments:
- tokens: bfloat16 [1024, 4096], P(('groups', 'feat'), 'tok'), parts along dimension 0, may hold values from -6 to 6
- out_grad: bfloat16 [1024, 4096], P(('groups', 'feat'), 'tok'), parts along dimension 0, may hold values from -0.75 to 0.75
- gate_weight: bfloat16 [4096, 14336], P('tok', 'feat'), may hold values from -0.09375 to 0.09375
- up_weight: bfloat16 [4096, 14336], P('tok', 'feat'), may hold values from -0.09375 to 0.09375
- down_weight: bfloat16 [14336, 4096], P('feat', 'tok'), may hold values from -0.046875 to 0.046875
Outputs:
- grad_gate: bfloat16 [8192, 14336], P(('groups', 'tok'), 'feat'), parts along dimension 0
- grad_up: bfloat16 [8192, 14336], P(('groups', 'tok'), 'feat'), parts along dimension 0
- grad_down: bfloat16 [28672, 4096], P(('groups', 'feat'), 'tok'), parts along dimension 0
The draws below stay inside these ranges and needn't reach their ends.
There are 2 independent parts, one for each index of `groups`. The reference program is written for one: setup_inputs(seed, part) draws one part's arguments, and reference() takes and returns one part's arrays. A program takes and returns all parts, laid end to end along the dimension named above; an argument that names none is the same for every part. Nothing has to cross between parts.
All inputs are finite; a program needn't handle non-finite values.
Results may differ from the reference program's by a relative error of at most 0.005.
Values may be sent and summed in bfloat16 or wider, within the bound.
A program may use at most 128 MiB of HBM per device.

```python
import jax
import jax.numpy as jnp

D = 4096
FF = 14336
TOKENS = 512


def levels(key, dims, cuts, low, top_value):
    gain = 1.0
    for dim, parts in cuts:
        steps = jax.random.uniform(jax.random.fold_in(jax.random.fold_in(key, 6), dim), (parts,), jnp.float32, low / len(cuts), top_value / len(cuts))
        gain = gain * jnp.repeat(jnp.exp(steps), dims[dim] // parts).reshape((-1,) + (1,) * (len(dims) - 1 - dim))
    return gain


def normal_values(stream_key, dims, scale, bound, cuts=(), kind=jnp.bfloat16):
    entries = jax.random.normal(stream_key, dims, jnp.float32) * scale
    if len(cuts) > 0:
        entries = levels(stream_key, dims, cuts, -0.22, 0.18) * entries
    return jnp.clip(entries, min=-bound, max=bound).astype(kind)


def setup_inputs(seed: int = 0, part: int = 0) -> dict:
    key_of = jax.random.split(jax.random.key(seed), 6)
    own_keys = jax.random.split(jax.random.fold_in(key_of[5], part), 6)
    return {
        "tokens": normal_values(own_keys[0], (TOKENS, D), 1.0, 6.0, ((0, 8), (1, 2))),
        "out_grad": normal_values(own_keys[1], (TOKENS, D), 0.125, 0.75, ((0, 8), (1, 2))),
        "gate_weight": normal_values(key_of[2], (D, FF), D ** -0.5, 0.09375, ((0, 2), (1, 8))),
        "up_weight": normal_values(key_of[3], (D, FF), D ** -0.5, 0.09375, ((0, 2), (1, 8))),
        "down_weight": normal_values(key_of[4], (FF, D), FF ** -0.5, 0.046875, ((0, 8), (1, 2))),
    }


def swiglu_parts(gate, up, grad_hidden):
    sigmoid_gate = jax.nn.sigmoid(gate)
    activated = gate * sigmoid_gate
    hidden = (activated * up).astype(jnp.bfloat16)
    gate_delta = (grad_hidden * up * sigmoid_gate * (1.0 + gate * (1.0 - sigmoid_gate))).astype(jnp.bfloat16)
    up_delta = (grad_hidden * activated).astype(jnp.bfloat16)
    return hidden, gate_delta, up_delta


def reference(tokens, out_grad, gate_weight, up_weight, down_weight):
    gate = jnp.dot(tokens, gate_weight, preferred_element_type=jnp.float32)
    up = jnp.dot(tokens, up_weight, preferred_element_type=jnp.float32)
    grad_hidden = jnp.dot(out_grad, down_weight.T, preferred_element_type=jnp.float32)
    hidden, gate_delta, up_delta = swiglu_parts(gate, up, grad_hidden)
    grad_gate = jnp.dot(tokens.T, gate_delta, preferred_element_type=jnp.float32).astype(jnp.bfloat16)
    grad_up = jnp.dot(tokens.T, up_delta, preferred_element_type=jnp.float32).astype(jnp.bfloat16)
    grad_down = jnp.dot(hidden.T, out_grad, preferred_element_type=jnp.float32).astype(jnp.bfloat16)
    return (grad_gate, grad_up, grad_down)
```

```python
import functools

import jax
import jax.numpy as jnp
from jax import lax
from jax.experimental import pallas as pl
from jax.experimental.pallas import tpu as pltpu
from jax.sharding import PartitionSpec as P

CHUNK = 256
VMEM_LIMIT = 48 * 1024 * 1024
F32, BF16 = jnp.float32, jnp.bfloat16


def contract_rows(left, right):
    return lax.dot_general(
        left, right, (((0,), (0,)), ((), ())), preferred_element_type=jnp.float32
    )


def swiglu_parts(gate, up, grad_hidden):
    sigmoid_gate = jax.nn.sigmoid(gate)
    activated = gate * sigmoid_gate
    hidden = (activated * up).astype(jnp.bfloat16)
    gate_delta = (grad_hidden * up * sigmoid_gate * (1.0 + gate * (1.0 - sigmoid_gate))).astype(
        jnp.bfloat16
    )
    up_delta = (grad_hidden * activated).astype(jnp.bfloat16)
    return (hidden, gate_delta, up_delta)


def plain_shards(tokens, out_grad, gate_weight, up_weight, down_weight):
    token_rows, grad_rows = (
        lax.all_gather(tokens, "feat", axis=0, tiled=True),
        lax.all_gather(out_grad, "feat", axis=0, tiled=True),
    )
    gate_part = jnp.dot(token_rows, gate_weight, preferred_element_type=jnp.float32)
    up_part = jnp.dot(token_rows, up_weight, preferred_element_type=jnp.float32)
    hidden_part = lax.dot_general(
        grad_rows, down_weight, (((1,), (1,)), ((), ())), preferred_element_type=jnp.float32
    )
    gate, up, grad_hidden = (
        lax.psum_scatter(part, "tok", scatter_dimension=0, tiled=True)
        for part in (gate_part, up_part, hidden_part)
    )
    hidden, gate_delta, up_delta = (
        lax.all_gather(part, "tok", axis=0, tiled=True)
        for part in swiglu_parts(gate, up, grad_hidden)
    )
    grad_gate = contract_rows(token_rows, gate_delta).astype(jnp.bfloat16)
    grad_up = contract_rows(token_rows, up_delta).astype(jnp.bfloat16)
    grad_down = contract_rows(hidden, grad_rows).astype(jnp.bfloat16)
    return (grad_gate, grad_up, grad_down)


def partial_kernel(n_token, n_grad, *refs):
    refs = list(refs)
    x_ref = refs.pop(0) if n_token else None
    w_refs = [refs.pop(0) for _ in range(n_token)]
    g_ref = refs.pop(0) if n_grad else None
    d_refs = [refs.pop(0) for _ in range(n_grad)]
    own_ref, send_ref = refs[-2:]
    for i, w_ref in enumerate(w_refs):
        part = jnp.dot(x_ref[...], w_ref[...], preferred_element_type=F32)
        own_ref[i] = part
        send_ref[i] = part.astype(BF16)
    for i, d_ref in enumerate(d_refs):
        part = lax.dot_general(
            g_ref[...], d_ref[...], (((1,), (1,)), ((), ())), preferred_element_type=F32
        )
        own_ref[n_token + i] = part
        send_ref[n_token + i] = part.astype(BF16)


def partial_products(rows, grad_rows, n_rows, weights, down, first, count, after):
    n_token, n_grad = len(weights), 0 if down is None else 1
    any_rows = rows if n_token else grad_rows
    depth = any_rows.shape[1]
    args, specs = [], []
    if n_token:
        args.append(rows)
        specs.append(pl.BlockSpec((n_rows, depth), lambda i: (0, 0)))
        for w in weights:
            args.append(w)
            specs.append(pl.BlockSpec((depth, CHUNK), lambda i: (0, first + i)))
    if n_grad:
        args.append(grad_rows)
        specs.append(pl.BlockSpec((n_rows, depth), lambda i: (0, 0)))
        args.append(down)
        specs.append(pl.BlockSpec((CHUNK, depth), lambda i: (first + i, 0)))
    for a in after:
        args.append(a)
        specs.append(pl.BlockSpec(memory_space=pl.ANY))
    n = n_token + n_grad
    block = pl.BlockSpec((n, n_rows, CHUNK), lambda i: (0, 0, i))
    shape = (n, n_rows, count * CHUNK)
    return pl.pallas_call(
        functools.partial(partial_kernel, n_token, n_grad),
        grid=(count,),
        in_specs=specs,
        out_specs=[block, block],
        out_shape=[jax.ShapeDtypeStruct(shape, F32), jax.ShapeDtypeStruct(shape, BF16)],
        compiler_params=pltpu.CompilerParams(vmem_limit_bytes=VMEM_LIMIT),
        cost_estimate=pl.CostEstimate(
            flops=2 * n * n_rows * depth * count * CHUNK,
            bytes_accessed=n * count * CHUNK * (2 * depth + 6 * n_rows) + 2 * n_rows * depth,
            transcendentals=0,
        ),
    )(*args)


def join_kernel(*refs):
    out_ref, base = refs[-1], 0
    for ref in refs[:-1]:
        n = ref.shape[0]
        out_ref[base : base + n, :] = ref[...]
        base += n


def join(pieces):
    n_rows = sum(p.shape[0] for p in pieces)
    depth = pieces[0].shape[1]
    tile = depth // 4
    return pl.pallas_call(
        join_kernel,
        grid=(4,),
        in_specs=[pl.BlockSpec((p.shape[0], tile), lambda i: (0, i)) for p in pieces],
        out_specs=pl.BlockSpec((n_rows, tile), lambda i: (0, i)),
        out_shape=jax.ShapeDtypeStruct((n_rows, depth), BF16),
        cost_estimate=pl.CostEstimate(
            flops=0, bytes_accessed=4 * n_rows * depth, transcendentals=0
        ),
    )(*pieces)


def flip_kernel(x_ref, *refs):
    refs[-1][...] = x_ref[...].T


def flip(x, after):
    n_rows, depth = x.shape
    tile = depth // 4
    return pl.pallas_call(
        flip_kernel,
        grid=(4,),
        in_specs=[pl.BlockSpec((n_rows, tile), lambda i: (0, i))]
        + [pl.BlockSpec(memory_space=pl.ANY)] * len(after),
        out_specs=pl.BlockSpec((tile, n_rows), lambda i: (i, 0)),
        out_shape=jax.ShapeDtypeStruct((depth, n_rows), BF16),
        cost_estimate=pl.CostEstimate(
            flops=0, bytes_accessed=4 * n_rows * depth, transcendentals=0
        ),
    )(x, *after)


def grads_kernel(
    own_a, got_a, own_b, got_b, own_t, got_t, own_g, got_g, flipped, grads, *rest
):
    gg_ref, gu_ref, gd_ref, hidden_t, gate_delta, up_delta = rest[-6:]

    @pl.when(pl.program_id(0) == 0)
    def _():
        base = 0
        for gate, up, grad_hidden in (
            (
                own_t[0] + got_t[0].astype(F32),
                own_t[1] + got_t[1].astype(F32),
                own_g[0] + got_g[0].astype(F32),
            ),
            tuple(own_a[i] + got_a[i].astype(F32) for i in range(3)),
            tuple(own_b[i] + got_b[i].astype(F32) for i in range(3)),
        ):
            sigmoid_gate = jax.nn.sigmoid(gate)
            activated = gate * sigmoid_gate
            n = gate.shape[0]
            hidden_t[:, base : base + n] = (activated * up).T.astype(BF16)
            gate_delta[base : base + n, :] = (
                grad_hidden * up * sigmoid_gate * (1.0 + gate * (1.0 - sigmoid_gate))
            ).astype(BF16)
            up_delta[base : base + n, :] = (grad_hidden * activated).astype(BF16)
            base += n

    gg_ref[...] = jnp.dot(flipped[...], gate_delta[...], preferred_element_type=F32).astype(BF16)
    gu_ref[...] = jnp.dot(flipped[...], up_delta[...], preferred_element_type=F32).astype(BF16)
    gd_ref[...] = jnp.dot(hidden_t[...], grads[...], preferred_element_type=F32).astype(BF16)


def chunk_grads(j, a, ja, b, jb, t, g, flipped, grads, hidden_units, so_far, after):
    depth, n_tokens = flipped.shape
    steps = 4
    tile = depth // steps

    def part(arr, k):
        return pl.BlockSpec((arr.shape[0], arr.shape[1], CHUNK), lambda i: (0, 0, k))

    args = [a[0], a[1], b[0], b[1], t[0], t[1], g[0], g[1], flipped, grads]
    specs = [part(a[0], ja), part(a[1], ja), part(b[0], jb), part(b[1], jb)]
    specs += [part(t[0], 0), part(t[1], 0), part(g[0], 0), part(g[1], 0)]
    specs += [
        pl.BlockSpec((tile, n_tokens), lambda i: (i, 0)),
        pl.BlockSpec((n_tokens, tile), lambda i: (0, i)),
    ]
    aliases = {}
    if so_far is not None:
        for k, arr in enumerate(so_far):
            aliases[len(args)] = k
            args.append(arr)
            specs.append(pl.BlockSpec(memory_space=pl.ANY))
    for arr in after:
        args.append(arr)
        specs.append(pl.BlockSpec(memory_space=pl.ANY))
    up_shape = jax.ShapeDtypeStruct((depth, hidden_units), BF16)
    down_shape = jax.ShapeDtypeStruct((hidden_units, depth), BF16)
    return pl.pallas_call(
        grads_kernel,
        grid=(steps,),
        in_specs=specs,
        out_specs=[
            pl.BlockSpec((tile, CHUNK), lambda i: (i, j)),
            pl.BlockSpec((tile, CHUNK), lambda i: (i, j)),
            pl.BlockSpec((CHUNK, tile), lambda i: (j, i)),
        ],
        out_shape=[up_shape, up_shape, down_shape],
        scratch_shapes=[
            pltpu.VMEM((CHUNK, n_tokens), BF16),
            pltpu.VMEM((n_tokens, CHUNK), BF16),
            pltpu.VMEM((n_tokens, CHUNK), BF16),
        ],
        input_output_aliases=aliases,
        compiler_params=pltpu.CompilerParams(vmem_limit_bytes=VMEM_LIMIT),
        cost_estimate=pl.CostEstimate(
            flops=6 * n_tokens * depth * CHUNK,
            bytes_accessed=4 * n_tokens * depth + 18 * n_tokens * CHUNK + 6 * depth * CHUNK,
            transcendentals=n_tokens * CHUNK,
        ),
    )(*args)


def pair_shards(n_feat, tokens, out_grad, gate_weight, up_weight, down_weight):
    hidden_units = gate_weight.shape[1]
    n_chunks = hidden_units // CHUNK
    weights = (gate_weight, up_weight)

    def swap(x):
        return lax.ppermute(x, "tok", [(0, 1), (1, 0)])

    def sibling(x):
        return lax.ppermute(x, "feat", [(i, i ^ 1) for i in range(n_feat)])

    def gather(x):
        got = [
            lax.ppermute(x, "feat", [(i, (i + k) % n_feat) for i in range(n_feat)])
            for k in range(2, n_feat, 2)
        ]
        return got + [sibling(piece) for piece in got]

    lead = 2
    n_own = tokens.shape[0]
    partial = partial_products
    own1, send1 = partial(tokens, out_grad, n_own, weights, down_weight, 0, lead, ())
    got1 = swap(send1)
    sib_tokens, sib_grad = sibling(tokens), sibling(out_grad)
    all_tokens = join(gather(tokens) + [tokens, sib_tokens])
    all_grad = join(gather(out_grad) + [out_grad, sib_grad])
    n_rest = all_tokens.shape[0] - 2 * n_own
    own2, send2 = partial(
        tokens, out_grad, n_own, weights, down_weight, lead, n_chunks - lead, (own1,)
    )
    got2 = swap(send2)
    own3, send3 = partial(
        sib_tokens, sib_grad, n_own, weights, down_weight, 0, n_chunks, (own2, got1)
    )
    got3 = swap(send3)

    t_parts, g_parts = [], []
    order = [("t", 0), ("t", 1), ("g", 0), ("g", 1)]
    for j in range(2, n_chunks):
        order += [("t", j), ("g", j)]
    gots = [got1, got2, got3]
    last = own3
    for kind, j in order:
        after = (last, gots[-3])
        if kind == "t":
            own, send = partial(all_tokens, None, n_rest, weights, None, j, 1, after)
        else:
            own, send = partial(None, all_grad, n_rest, (), down_weight, j, 1, after)
        last = own
        got = swap(send)
        gots.append(got)
        (t_parts if kind == "t" else g_parts).append((own, got))

    flipped = flip(all_tokens, (t_parts[1][0],))
    outs = None
    for j in range(n_chunks):
        a, ja = ((own1, got1), j) if j < lead else ((own2, got2), j - lead)
        after = (g_parts[j + 2][0],) if j + 2 < n_chunks else ()
        outs = chunk_grads(
            j, a, ja, (own3, got3), j, t_parts[j], g_parts[j], flipped, all_grad,
            hidden_units, outs, after,
        )
    return tuple(outs)


def solution(mesh):
    n_feat, n_tok = mesh.shape["feat"], mesh.shape["tok"]
    pair = n_tok == 2 and n_feat % 2 == 0 and 2 < n_feat <= 8
    return jax.shard_map(
        functools.partial(pair_shards, n_feat) if pair else plain_shards,
        mesh=mesh,
        in_specs=(
            P(("groups", "feat"), "tok"),
            P(("groups", "feat"), "tok"),
            P("tok", "feat"),
            P("tok", "feat"),
            P("feat", "tok"),
        ),
        out_specs=(
            P(("groups", "tok"), "feat"),
            P(("groups", "tok"), "feat"),
            P(("groups", "feat"), "tok"),
        ),
        check_vma=False,
    )
```

```python
import functools

import jax
import jax.numpy as jnp
from jax import lax
from jax.experimental import pallas as pl
from jax.experimental.pallas import tpu as pltpu
from jax.sharding import PartitionSpec as P

CHUNK = 256
VMEM_LIMIT = 48 * 1024 * 1024
F32, BF16 = jnp.float32, jnp.bfloat16
SMALL_COST = pl.CostEstimate(flops=1024, bytes_accessed=1024, transcendentals=0)


def contract_rows(left, right):
    return lax.dot_general(
        left, right, (((0,), (0,)), ((), ())), preferred_element_type=jnp.float32
    )


def swiglu_parts(gate, up, grad_hidden):
    sigmoid_gate = jax.nn.sigmoid(gate)
    activated = gate * sigmoid_gate
    hidden = (activated * up).astype(jnp.bfloat16)
    gate_delta = (grad_hidden * up * sigmoid_gate * (1.0 + gate * (1.0 - sigmoid_gate))).astype(
        jnp.bfloat16
    )
    up_delta = (grad_hidden * activated).astype(jnp.bfloat16)
    return (hidden, gate_delta, up_delta)


def plain_shards(tokens, out_grad, gate_weight, up_weight, down_weight):
    token_rows, grad_rows = (
        lax.all_gather(tokens, "feat", axis=0, tiled=True),
        lax.all_gather(out_grad, "feat", axis=0, tiled=True),
    )
    gate_part = jnp.dot(token_rows, gate_weight, preferred_element_type=jnp.float32)
    up_part = jnp.dot(token_rows, up_weight, preferred_element_type=jnp.float32)
    hidden_part = lax.dot_general(
        grad_rows, down_weight, (((1,), (1,)), ((), ())), preferred_element_type=jnp.float32
    )
    gate, up, grad_hidden = (
        lax.psum_scatter(part, "tok", scatter_dimension=0, tiled=True)
        for part in (gate_part, up_part, hidden_part)
    )
    hidden, gate_delta, up_delta = (
        lax.all_gather(part, "tok", axis=0, tiled=True)
        for part in swiglu_parts(gate, up, grad_hidden)
    )
    grad_gate = contract_rows(token_rows, gate_delta).astype(jnp.bfloat16)
    grad_up = contract_rows(token_rows, up_delta).astype(jnp.bfloat16)
    grad_down = contract_rows(hidden, grad_rows).astype(jnp.bfloat16)
    return (grad_gate, grad_up, grad_down)


def rows_of(refs):
    parts = [ref[...] for ref in refs]
    return parts[0] if len(parts) == 1 else jnp.concatenate(parts, axis=0)


def partial_kernel(n_pieces, n_token, n_grad, *refs):
    refs = list(refs)
    own_ref, send_ref = refs[-2:]
    if n_token:
        rows = rows_of([refs.pop(0) for _ in range(n_pieces)])
        for i in range(n_token):
            part = jnp.dot(rows, refs.pop(0)[...], preferred_element_type=F32)
            own_ref[i] = part
            send_ref[i] = part.astype(BF16)
    if n_grad:
        rows = rows_of([refs.pop(0) for _ in range(n_pieces)])
        part = lax.dot_general(
            rows, refs.pop(0)[...], (((1,), (1,)), ((), ())), preferred_element_type=F32
        )
        own_ref[n_token] = part
        send_ref[n_token] = part.astype(BF16)


def partial_products(rows, grad_rows, heights, weights, down, first, width, after):
    n_token, n_grad = len(weights), 0 if down is None else 1
    n_rows = sum(heights)
    depth = (rows or grad_rows)[0].shape[1]
    start, count = first // CHUNK, width // CHUNK
    piece_specs = [pl.BlockSpec((h, depth), lambda i: (0, 0)) for h in heights]
    args, specs = [], []
    if n_token:
        args += rows
        specs += piece_specs
        for w in weights:
            args.append(w)
            specs.append(pl.BlockSpec((depth, CHUNK), lambda i: (0, start + i)))
    if n_grad:
        args += grad_rows
        specs += piece_specs
        args.append(down)
        specs.append(pl.BlockSpec((CHUNK, depth), lambda i: (start + i, 0)))
    for a in after:
        args.append(a)
        specs.append(pl.BlockSpec(memory_space=pl.ANY))
    n = n_token + n_grad
    block = pl.BlockSpec((n, n_rows, CHUNK), lambda i: (0, 0, i))
    shape = (n, n_rows, width)
    return pl.pallas_call(
        functools.partial(partial_kernel, len(heights), n_token, n_grad),
        grid=(count,),
        in_specs=specs,
        out_specs=[block, block],
        out_shape=[jax.ShapeDtypeStruct(shape, F32), jax.ShapeDtypeStruct(shape, BF16)],
        compiler_params=pltpu.CompilerParams(vmem_limit_bytes=VMEM_LIMIT),
        cost_estimate=SMALL_COST,
    )(*args)


def join_kernel(n_pieces, n_after, *refs):
    refs = refs[:n_pieces] + refs[n_pieces + n_after :]
    out_ref, base = refs[n_pieces], 0
    for ref in refs[:n_pieces]:
        n = ref.shape[0]
        out_ref[base : base + n, :] = ref[...]
        base += n
    if len(refs) > n_pieces + 1:
        refs[-1][...] = out_ref[...].T


def join(pieces, flip, after):
    n_rows = sum(p.shape[0] for p in pieces)
    depth = pieces[0].shape[1]
    tile = depth // 2
    out_specs = [pl.BlockSpec((n_rows, tile), lambda i: (0, i))]
    out_shape = [jax.ShapeDtypeStruct((n_rows, depth), BF16)]
    if flip:
        out_specs.append(pl.BlockSpec((tile, n_rows), lambda i: (i, 0)))
        out_shape.append(jax.ShapeDtypeStruct((depth, n_rows), BF16))
    return pl.pallas_call(
        functools.partial(join_kernel, len(pieces), len(after)),
        grid=(2,),
        in_specs=[pl.BlockSpec((p.shape[0], tile), lambda i: (0, i)) for p in pieces]
        + [pl.BlockSpec(memory_space=pl.ANY)] * len(after),
        out_specs=out_specs,
        out_shape=out_shape,
        compiler_params=pltpu.CompilerParams(vmem_limit_bytes=VMEM_LIMIT),
        cost_estimate=SMALL_COST,
    )(*pieces, *after)


def others_kernel(n_own, blocks_ref, *refs):
    n_chips = blocks_ref.shape[0] // n_own
    chip = lax.axis_index("feat") // 2
    for k in range(1, n_chips):
        row = pl.multiple_of(lax.rem(chip + k, n_chips) * n_own, n_own)
        refs[-1][(k - 1) * n_own : k * n_own, :] = blocks_ref[pl.ds(row, n_own), :]


def others(blocks, n_own, after):
    n_rows, depth = blocks.shape
    tile = depth // 2
    return pl.pallas_call(
        functools.partial(others_kernel, n_own),
        grid=(2,),
        in_specs=[pl.BlockSpec((n_rows, tile), lambda i: (0, i))]
        + [pl.BlockSpec(memory_space=pl.ANY)] * len(after),
        out_specs=pl.BlockSpec((n_rows - n_own, tile), lambda i: (0, i)),
        out_shape=jax.ShapeDtypeStruct((n_rows - n_own, depth), BF16),
        compiler_params=pltpu.CompilerParams(vmem_limit_bytes=VMEM_LIMIT),
        cost_estimate=SMALL_COST,
    )(blocks, *after)


def grads_kernel(own_a, got_a, own_t, got_t, own_g, got_g, flipped, grads, *rest):
    gg_ref, gu_ref, gd_ref, hidden_t, gate_delta, up_delta = rest[-6:]

    @pl.when(pl.program_id(0) == 0)
    def _():
        def total(own, got, i):
            return own[i] + got[i].astype(F32)

        base = 0
        for gate, up, grad_hidden in (
            (
                total(own_t, got_t, 0),
                total(own_t, got_t, 1),
                total(own_g, got_g, own_g.shape[0] - 1),
            ),
            tuple(total(own_a, got_a, i) for i in range(3)),
        ):
            sigmoid_gate = jax.nn.sigmoid(gate)
            activated = gate * sigmoid_gate
            n = gate.shape[0]
            hidden_t[:, base : base + n] = (activated * up).astype(BF16).T
            gate_delta[base : base + n, :] = (
                grad_hidden * up * sigmoid_gate * (1.0 + gate * (1.0 - sigmoid_gate))
            ).astype(BF16)
            up_delta[base : base + n, :] = (grad_hidden * activated).astype(BF16)
            base += n

    gg_ref[...] = jnp.dot(flipped[...], gate_delta[...], preferred_element_type=F32).astype(BF16)
    gu_ref[...] = jnp.dot(flipped[...], up_delta[...], preferred_element_type=F32).astype(BF16)
    gd_ref[...] = jnp.dot(hidden_t[...], grads[...], preferred_element_type=F32).astype(BF16)


def group_grads(
    first, width, a, a_first, t, g, far_first, flipped, grads, hidden_units, so_far, after
):
    depth, n_tokens = flipped.shape
    steps = 4
    tile = depth // steps
    j, far = first // width, far_first // width

    def part(arr, offset):
        return pl.BlockSpec(
            (arr.shape[0], arr.shape[1], width), lambda i: (0, 0, offset // width)
        )

    g_block = pl.BlockSpec((1, g[0].shape[1], width), lambda i: (g[0].shape[0] - 1, 0, far))
    t_block = pl.BlockSpec((2, t[0].shape[1], width), lambda i: (0, 0, far))
    args = [a[0], a[1], t[0], t[1], g[0], g[1], flipped, grads]
    specs = [part(a[0], a_first), part(a[1], a_first), t_block, t_block, g_block, g_block]
    specs += [
        pl.BlockSpec((tile, n_tokens), lambda i: (i, 0)),
        pl.BlockSpec((n_tokens, tile), lambda i: (0, i)),
    ]
    aliases = {}
    if so_far is not None:
        for k, arr in enumerate(so_far):
            aliases[len(args)] = k
            args.append(arr)
            specs.append(pl.BlockSpec(memory_space=pl.ANY))
    for arr in after:
        args.append(arr)
        specs.append(pl.BlockSpec(memory_space=pl.ANY))
    up_shape = jax.ShapeDtypeStruct((depth, hidden_units), BF16)
    down_shape = jax.ShapeDtypeStruct((hidden_units, depth), BF16)
    return pl.pallas_call(
        grads_kernel,
        grid=(steps,),
        in_specs=specs,
        out_specs=[
            pl.BlockSpec((tile, width), lambda i: (i, j)),
            pl.BlockSpec((tile, width), lambda i: (i, j)),
            pl.BlockSpec((width, tile), lambda i: (j, i)),
        ],
        out_shape=[up_shape, up_shape, down_shape],
        scratch_shapes=[
            pltpu.VMEM((width, n_tokens), BF16),
            pltpu.VMEM((n_tokens, width), BF16),
            pltpu.VMEM((n_tokens, width), BF16),
        ],
        input_output_aliases=aliases,
        compiler_params=pltpu.CompilerParams(vmem_limit_bytes=VMEM_LIMIT),
        cost_estimate=SMALL_COST,
    )(*args)


def pair_shards(n_feat, tokens, out_grad, gate_weight, up_weight, down_weight):
    hidden_units = gate_weight.shape[1]
    weights = (gate_weight, up_weight)
    wide = 2 * CHUNK
    n_own = tokens.shape[0]
    partial = partial_products

    def swap(x):
        return lax.ppermute(x, "tok", [(0, 1), (1, 0)])

    def sibling(x):
        return lax.ppermute(x, "feat", [(i, i ^ 1) for i in range(n_feat)])

    def gather(x):
        return lax.all_gather(
            x, "feat", axis=0, tiled=True,
            axis_index_groups=[list(range(c, n_feat, 2)) for c in range(2)],
        )

    near_tokens = [tokens, sibling(tokens)]
    near_grad = [out_grad, sibling(out_grad)]
    token_blocks, grad_blocks = gather(tokens), gather(out_grad)
    near = (n_own, n_own)
    far = ((n_feat - 2) * n_own,)

    def near_part(first, width, after):
        own, send = partial(
            near_tokens, near_grad, near, weights, down_weight, first, width, after
        )
        return own, swap(send)

    def far_part(first, width, kinds, after):
        own, send = partial(
            [all_tokens] if "t" in kinds else None,
            [all_grad] if "g" in kinds else None,
            far,
            weights if "t" in kinds else (),
            down_weight if "g" in kinds else None,
            first, width, after,
        )
        return own, swap(send)

    def joined(blocks, near_pieces, flip, after):
        mine = others(blocks, n_own, after)
        return join([mine, sibling(mine)] + near_pieces, flip, ())

    a0 = near_part(0, wide, ())
    a1 = near_part(wide, hidden_units - wide, (a0[0],))
    all_tokens, flipped = joined(token_blocks, near_tokens, True, (a1[0], a0[1]))
    t0 = far_part(0, wide, "t", (a1[1],))
    t1 = far_part(wide, wide, "t", (t0[0],))
    all_grad = joined(grad_blocks, near_grad, False, (t1[0], t0[1]))[0]
    g0 = far_part(0, wide, "g", (t1[0],))
    g1 = far_part(wide, wide, "g", (g0[0], t1[1]))
    f2 = far_part(2 * wide, wide, "tg", (g1[0], g0[1]))
    f3 = far_part(3 * wide, hidden_units - 3 * wide, "tg", (f2[0], g1[1]))

    outs = None
    for first, width, a, a_first, t, g, far_first, after in (
        (0, wide, a0, 0, t0, g0, 0, (f2[0],)),
        (wide, wide, a1, 0, t1, g1, 0, (f3[0],)),
        (2 * wide, wide, a1, wide, f2, f2, 0, ()),
        (3 * wide, hidden_units - 3 * wide, a1, 2 * wide, f3, f3, 0, ()),
    ):
        outs = group_grads(
            first, width, a, a_first, t, g, far_first, flipped, all_grad, hidden_units,
            outs, after,
        )
    return tuple(outs)


def solution(mesh):
    n_feat, n_tok = mesh.shape["feat"], mesh.shape["tok"]
    pair = n_tok == 2 and n_feat % 2 == 0 and 2 < n_feat <= 8
    return jax.shard_map(
        functools.partial(pair_shards, n_feat) if pair else plain_shards,
        mesh=mesh,
        in_specs=(
            P(("groups", "feat"), "tok"),
            P(("groups", "feat"), "tok"),
            P("tok", "feat"),
            P("tok", "feat"),
            P("feat", "tok"),
        ),
        out_specs=(
            P(("groups", "tok"), "feat"),
            P(("groups", "tok"), "feat"),
            P(("groups", "feat"), "tok"),
        ),
        check_vma=False,
    )
```

```python
import functools

import jax
import jax.numpy as jnp
from jax import lax
from jax.experimental import pallas as pl
from jax.experimental.pallas import tpu as pltpu
from jax.sharding import PartitionSpec as P

CHUNK = 256
VMEM_LIMIT = 48 * 1024 * 1024
F32, BF16 = jnp.float32, jnp.bfloat16
SMALL_COST = pl.CostEstimate(flops=1024, bytes_accessed=1024, transcendentals=0)


def contract_rows(left, right):
    return lax.dot_general(
        left, right, (((0,), (0,)), ((), ())), preferred_element_type=jnp.float32
    )


def swiglu_parts(gate, up, grad_hidden):
    sigmoid_gate = jax.nn.sigmoid(gate)
    activated = gate * sigmoid_gate
    hidden = (activated * up).astype(jnp.bfloat16)
    gate_delta = (grad_hidden * up * sigmoid_gate * (1.0 + gate * (1.0 - sigmoid_gate))).astype(
        jnp.bfloat16
    )
    up_delta = (grad_hidden * activated).astype(jnp.bfloat16)
    return (hidden, gate_delta, up_delta)


def plain_shards(tokens, out_grad, gate_weight, up_weight, down_weight):
    token_rows, grad_rows = (
        lax.all_gather(tokens, "feat", axis=0, tiled=True),
        lax.all_gather(out_grad, "feat", axis=0, tiled=True),
    )
    gate_part = jnp.dot(token_rows, gate_weight, preferred_element_type=jnp.float32)
    up_part = jnp.dot(token_rows, up_weight, preferred_element_type=jnp.float32)
    hidden_part = lax.dot_general(
        grad_rows, down_weight, (((1,), (1,)), ((), ())), preferred_element_type=jnp.float32
    )
    gate, up, grad_hidden = (
        lax.psum_scatter(part, "tok", scatter_dimension=0, tiled=True)
        for part in (gate_part, up_part, hidden_part)
    )
    hidden, gate_delta, up_delta = (
        lax.all_gather(part, "tok", axis=0, tiled=True)
        for part in swiglu_parts(gate, up, grad_hidden)
    )
    grad_gate = contract_rows(token_rows, gate_delta).astype(jnp.bfloat16)
    grad_up = contract_rows(token_rows, up_delta).astype(jnp.bfloat16)
    grad_down = contract_rows(hidden, grad_rows).astype(jnp.bfloat16)
    return (grad_gate, grad_up, grad_down)


def rows_of(refs):
    parts = [ref[...] for ref in refs]
    return parts[0] if len(parts) == 1 else jnp.concatenate(parts, axis=0)


def partial_kernel(n_pieces, n_token, n_grad, *refs):
    refs = list(refs)
    own_ref, send_ref = refs[-2:]
    if n_token:
        rows = rows_of([refs.pop(0) for _ in range(n_pieces)])
        for i in range(n_token):
            part = jnp.dot(rows, refs.pop(0)[...], preferred_element_type=F32)
            own_ref[i] = part
            send_ref[i] = part.astype(BF16)
    if n_grad:
        rows = rows_of([refs.pop(0) for _ in range(n_pieces)])
        part = lax.dot_general(
            rows, refs.pop(0)[...], (((1,), (1,)), ((), ())), preferred_element_type=F32
        )
        own_ref[n_token] = part
        send_ref[n_token] = part.astype(BF16)


def partial_products(rows, grad_rows, heights, weights, down, first, width, after):
    n_token, n_grad = len(weights), 0 if down is None else 1
    n_rows = sum(heights)
    depth = (rows or grad_rows)[0].shape[1]
    start, count = first // CHUNK, width // CHUNK
    piece_specs = [pl.BlockSpec((h, depth), lambda i: (0, 0)) for h in heights]
    args, specs = [], []
    if n_token:
        args += rows
        specs += piece_specs
        for w in weights:
            args.append(w)
            specs.append(pl.BlockSpec((depth, CHUNK), lambda i: (0, start + i)))
    if n_grad:
        args += grad_rows
        specs += piece_specs
        args.append(down)
        specs.append(pl.BlockSpec((CHUNK, depth), lambda i: (start + i, 0)))
    for a in after:
        args.append(a)
        specs.append(pl.BlockSpec(memory_space=pl.ANY))
    n = n_token + n_grad
    block = pl.BlockSpec((n, n_rows, CHUNK), lambda i: (0, 0, i))
    shape = (n, n_rows, width)
    return pl.pallas_call(
        functools.partial(partial_kernel, len(heights), n_token, n_grad),
        grid=(count,),
        in_specs=specs,
        out_specs=[block, block],
        out_shape=[jax.ShapeDtypeStruct(shape, F32), jax.ShapeDtypeStruct(shape, BF16)],
        compiler_params=pltpu.CompilerParams(vmem_limit_bytes=VMEM_LIMIT),
        cost_estimate=SMALL_COST,
    )(*args)


def join_kernel(n_pieces, n_after, *refs):
    refs = refs[:n_pieces] + refs[n_pieces + n_after :]
    out_ref, base = refs[n_pieces], 0
    for ref in refs[:n_pieces]:
        n = ref.shape[0]
        out_ref[base : base + n, :] = ref[...]
        base += n
    if len(refs) > n_pieces + 1:
        refs[-1][...] = out_ref[...].T


def join(pieces, flip, after):
    n_rows = sum(p.shape[0] for p in pieces)
    depth = pieces[0].shape[1]
    tile = depth // 2
    out_specs = [pl.BlockSpec((n_rows, tile), lambda i: (0, i))]
    out_shape = [jax.ShapeDtypeStruct((n_rows, depth), BF16)]
    if flip:
        out_specs.append(pl.BlockSpec((tile, n_rows), lambda i: (i, 0)))
        out_shape.append(jax.ShapeDtypeStruct((depth, n_rows), BF16))
    return pl.pallas_call(
        functools.partial(join_kernel, len(pieces), len(after)),
        grid=(2,),
        in_specs=[pl.BlockSpec((p.shape[0], tile), lambda i: (0, i)) for p in pieces]
        + [pl.BlockSpec(memory_space=pl.ANY)] * len(after),
        out_specs=out_specs,
        out_shape=out_shape,
        compiler_params=pltpu.CompilerParams(vmem_limit_bytes=VMEM_LIMIT),
        cost_estimate=SMALL_COST,
    )(*pieces, *after)


def others_kernel(n_own, blocks_ref, *refs):
    n_chips = blocks_ref.shape[0] // n_own
    chip = lax.axis_index("feat") // 2
    for k in range(1, n_chips):
        row = pl.multiple_of(lax.rem(chip + k, n_chips) * n_own, n_own)
        refs[-1][(k - 1) * n_own : k * n_own, :] = blocks_ref[pl.ds(row, n_own), :]


def others(blocks, n_own, after):
    n_rows, depth = blocks.shape
    tile = depth // 2
    return pl.pallas_call(
        functools.partial(others_kernel, n_own),
        grid=(2,),
        in_specs=[pl.BlockSpec((n_rows, tile), lambda i: (0, i))]
        + [pl.BlockSpec(memory_space=pl.ANY)] * len(after),
        out_specs=pl.BlockSpec((n_rows - n_own, tile), lambda i: (0, i)),
        out_shape=jax.ShapeDtypeStruct((n_rows - n_own, depth), BF16),
        compiler_params=pltpu.CompilerParams(vmem_limit_bytes=VMEM_LIMIT),
        cost_estimate=SMALL_COST,
    )(blocks, *after)


def grads_kernel(own_a, got_a, own_t, got_t, own_g, got_g, flipped, grads, *rest):
    gg_ref, gu_ref, gd_ref, hidden_t, gate_delta, up_delta = rest[-6:]

    @pl.when(pl.program_id(0) == 0)
    def _():
        def total(own, got, i):
            return own[i] + got[i].astype(F32)

        base = 0
        for gate, up, grad_hidden in (
            (
                total(own_t, got_t, 0),
                total(own_t, got_t, 1),
                total(own_g, got_g, own_g.shape[0] - 1),
            ),
            tuple(total(own_a, got_a, i) for i in range(3)),
        ):
            sigmoid_gate = jax.nn.sigmoid(gate)
            activated = gate * sigmoid_gate
            n = gate.shape[0]
            hidden_t[:, base : base + n] = (activated * up).astype(BF16).T
            gate_delta[base : base + n, :] = (
                grad_hidden * up * sigmoid_gate * (1.0 + gate * (1.0 - sigmoid_gate))
            ).astype(BF16)
            up_delta[base : base + n, :] = (grad_hidden * activated).astype(BF16)
            base += n

    gg_ref[...] = jnp.dot(flipped[...], gate_delta[...], preferred_element_type=F32).astype(BF16)
    gu_ref[...] = jnp.dot(flipped[...], up_delta[...], preferred_element_type=F32).astype(BF16)
    gd_ref[...] = jnp.dot(hidden_t[...], grads[...], preferred_element_type=F32).astype(BF16)


def group_grads(
    first, width, a, a_first, t, g, far_first, flipped, grads, hidden_units, so_far, after
):
    depth, n_tokens = flipped.shape
    steps = 4
    tile = depth // steps
    j, far = first // width, far_first // width

    def part(arr, offset):
        return pl.BlockSpec(
            (arr.shape[0], arr.shape[1], width), lambda i: (0, 0, offset // width)
        )

    g_block = pl.BlockSpec((1, g[0].shape[1], width), lambda i: (g[0].shape[0] - 1, 0, far))
    t_block = pl.BlockSpec((2, t[0].shape[1], width), lambda i: (0, 0, far))
    args = [a[0], a[1], t[0], t[1], g[0], g[1], flipped, grads]
    specs = [part(a[0], a_first), part(a[1], a_first), t_block, t_block, g_block, g_block]
    specs += [
        pl.BlockSpec((tile, n_tokens), lambda i: (i, 0)),
        pl.BlockSpec((n_tokens, tile), lambda i: (0, i)),
    ]
    aliases = {}
    if so_far is not None:
        for k, arr in enumerate(so_far):
            aliases[len(args)] = k
            args.append(arr)
            specs.append(pl.BlockSpec(memory_space=pl.ANY))
    for arr in after:
        args.append(arr)
        specs.append(pl.BlockSpec(memory_space=pl.ANY))
    up_shape = jax.ShapeDtypeStruct((depth, hidden_units), BF16)
    down_shape = jax.ShapeDtypeStruct((hidden_units, depth), BF16)
    return pl.pallas_call(
        grads_kernel,
        grid=(steps,),
        in_specs=specs,
        out_specs=[
            pl.BlockSpec((tile, width), lambda i: (i, j)),
            pl.BlockSpec((tile, width), lambda i: (i, j)),
            pl.BlockSpec((width, tile), lambda i: (j, i)),
        ],
        out_shape=[up_shape, up_shape, down_shape],
        scratch_shapes=[
            pltpu.VMEM((width, n_tokens), BF16),
            pltpu.VMEM((n_tokens, width), BF16),
            pltpu.VMEM((n_tokens, width), BF16),
        ],
        input_output_aliases=aliases,
        compiler_params=pltpu.CompilerParams(vmem_limit_bytes=VMEM_LIMIT),
        cost_estimate=SMALL_COST,
    )(*args)


def pair_shards(n_feat, tokens, out_grad, gate_weight, up_weight, down_weight):
    hidden_units = gate_weight.shape[1]
    weights = (gate_weight, up_weight)
    wide = 2 * CHUNK
    n_own = tokens.shape[0]
    partial = partial_products

    def swap(x):
        return lax.ppermute(x, "tok", [(0, 1), (1, 0)])

    def sibling(x):
        return lax.ppermute(x, "feat", [(i, i ^ 1) for i in range(n_feat)])

    def gather(x):
        return lax.all_gather(
            x, "feat", axis=0, tiled=True,
            axis_index_groups=[list(range(c, n_feat, 2)) for c in range(2)],
        )

    near_tokens = [tokens, sibling(tokens)]
    near_grad = [out_grad, sibling(out_grad)]
    token_blocks, grad_blocks = gather(tokens), gather(out_grad)
    near = (n_own, n_own)
    far = ((n_feat // 2 - 1) * n_own,) * 2

    def near_part(first, width, after):
        own, send = partial(
            near_tokens, near_grad, near, weights, down_weight, first, width, after
        )
        return own, swap(send)

    def far_part(first, width, kinds, after):
        own, send = partial(
            far_tokens if "t" in kinds else None,
            far_grad if "g" in kinds else None,
            far,
            weights if "t" in kinds else (),
            down_weight if "g" in kinds else None,
            first, width, after,
        )
        return own, swap(send)

    def far_rows(blocks, after):
        mine = others(blocks, n_own, after)
        return [mine, sibling(mine)]

    a0 = near_part(0, wide, ())
    a1 = near_part(wide, hidden_units - wide, (a0[0],))
    far_tokens = far_rows(token_blocks, (a1[0], a0[1]))
    t01 = far_part(0, 2 * wide, "t", (a1[1],))
    flipped = join(far_tokens + near_tokens, True, (t01[0],))[1]
    far_grad = far_rows(grad_blocks, (t01[0],))
    g01 = far_part(0, 2 * wide, "g", (t01[0],))
    all_grad = join(far_grad + near_grad, False, (g01[0],))[0]
    f2 = far_part(2 * wide, wide, "tg", (g01[0], t01[1]))
    f3 = far_part(3 * wide, hidden_units - 3 * wide, "tg", (f2[0], g01[1]))

    outs = None
    for first, width, a, a_first, t, g, after in (
        (0, wide, a0, 0, t01, g01, (f3[0],)),
        (wide, wide, a1, 0, t01, g01, ()),
        (2 * wide, wide, a1, wide, f2, f2, ()),
        (3 * wide, hidden_units - 3 * wide, a1, 2 * wide, f3, f3, ()),
    ):
        far_first = wide if first == wide else 0
        outs = group_grads(
            first, width, a, a_first, t, g, far_first, flipped, all_grad, hidden_units,
            outs, after,
        )
    return tuple(outs)


def solution(mesh):
    n_feat, n_tok = mesh.shape["feat"], mesh.shape["tok"]
    pair = n_tok == 2 and n_feat % 2 == 0 and 2 < n_feat <= 8
    return jax.shard_map(
        functools.partial(pair_shards, n_feat) if pair else plain_shards,
        mesh=mesh,
        in_specs=(
            P(("groups", "feat"), "tok"),
            P(("groups", "feat"), "tok"),
            P("tok", "feat"),
            P("tok", "feat"),
            P("feat", "tok"),
        ),
        out_specs=(
            P(("groups", "tok"), "feat"),
            P(("groups", "tok"), "feat"),
            P(("groups", "feat"), "tok"),
        ),
        check_vma=False,
    )
```

```python
import functools

import jax
import jax.numpy as jnp
from jax import lax
from jax.experimental import pallas as pl
from jax.experimental.pallas import tpu as pltpu
from jax.sharding import PartitionSpec as P

CHUNK = 256
VMEM_LIMIT = 48 * 1024 * 1024
F32, BF16 = jnp.float32, jnp.bfloat16
SMALL_COST = pl.CostEstimate(flops=1024, bytes_accessed=1024, transcendentals=0)


def contract_rows(left, right):
    return lax.dot_general(
        left, right, (((0,), (0,)), ((), ())), preferred_element_type=jnp.float32
    )


def swiglu_parts(gate, up, grad_hidden):
    sigmoid_gate = jax.nn.sigmoid(gate)
    activated = gate * sigmoid_gate
    hidden = (activated * up).astype(jnp.bfloat16)
    gate_delta = (grad_hidden * up * sigmoid_gate * (1.0 + gate * (1.0 - sigmoid_gate))).astype(
        jnp.bfloat16
    )
    up_delta = (grad_hidden * activated).astype(jnp.bfloat16)
    return (hidden, gate_delta, up_delta)


def plain_shards(tokens, out_grad, gate_weight, up_weight, down_weight):
    token_rows, grad_rows = (
        lax.all_gather(tokens, "feat", axis=0, tiled=True),
        lax.all_gather(out_grad, "feat", axis=0, tiled=True),
    )
    gate_part = jnp.dot(token_rows, gate_weight, preferred_element_type=jnp.float32)
    up_part = jnp.dot(token_rows, up_weight, preferred_element_type=jnp.float32)
    hidden_part = lax.dot_general(
        grad_rows, down_weight, (((1,), (1,)), ((), ())), preferred_element_type=jnp.float32
    )
    gate, up, grad_hidden = (
        lax.psum_scatter(part, "tok", scatter_dimension=0, tiled=True)
        for part in (gate_part, up_part, hidden_part)
    )
    hidden, gate_delta, up_delta = (
        lax.all_gather(part, "tok", axis=0, tiled=True)
        for part in swiglu_parts(gate, up, grad_hidden)
    )
    grad_gate = contract_rows(token_rows, gate_delta).astype(jnp.bfloat16)
    grad_up = contract_rows(token_rows, up_delta).astype(jnp.bfloat16)
    grad_down = contract_rows(hidden, grad_rows).astype(jnp.bfloat16)
    return (grad_gate, grad_up, grad_down)


def rows_of(refs):
    parts = [ref[...] for ref in refs]
    return parts[0] if len(parts) == 1 else jnp.concatenate(parts, axis=0)


def partial_kernel(n_pieces, n_token, n_grad, *refs):
    refs = list(refs)
    own_ref, send_ref = refs[-2:]
    if n_token:
        rows = rows_of([refs.pop(0) for _ in range(n_pieces)])
        for i in range(n_token):
            part = jnp.dot(rows, refs.pop(0)[...], preferred_element_type=F32)
            own_ref[i] = part
            send_ref[i] = part.astype(BF16)
    if n_grad:
        rows = rows_of([refs.pop(0) for _ in range(n_pieces)])
        part = lax.dot_general(
            rows, refs.pop(0)[...], (((1,), (1,)), ((), ())), preferred_element_type=F32
        )
        own_ref[n_token] = part
        send_ref[n_token] = part.astype(BF16)


def partial_products(rows, grad_rows, heights, weights, down, first, width, after):
    n_token, n_grad = len(weights), 0 if down is None else 1
    n_rows = sum(heights)
    depth = (rows or grad_rows)[0].shape[1]
    start, count = first // CHUNK, width // CHUNK
    piece_specs = [pl.BlockSpec((h, depth), lambda i: (0, 0)) for h in heights]
    args, specs = [], []
    if n_token:
        args += rows
        specs += piece_specs
        for w in weights:
            args.append(w)
            specs.append(pl.BlockSpec((depth, CHUNK), lambda i: (0, start + i)))
    if n_grad:
        args += grad_rows
        specs += piece_specs
        args.append(down)
        specs.append(pl.BlockSpec((CHUNK, depth), lambda i: (start + i, 0)))
    for a in after:
        args.append(a)
        specs.append(pl.BlockSpec(memory_space=pl.ANY))
    n = n_token + n_grad
    block = pl.BlockSpec((n, n_rows, CHUNK), lambda i: (0, 0, i))
    shape = (n, n_rows, width)
    return pl.pallas_call(
        functools.partial(partial_kernel, len(heights), n_token, n_grad),
        grid=(count,),
        in_specs=specs,
        out_specs=[block, block],
        out_shape=[jax.ShapeDtypeStruct(shape, F32), jax.ShapeDtypeStruct(shape, BF16)],
        compiler_params=pltpu.CompilerParams(vmem_limit_bytes=VMEM_LIMIT),
        cost_estimate=SMALL_COST,
    )(*args)


def join_kernel(n_pieces, n_after, *refs):
    refs = refs[:n_pieces] + refs[n_pieces + n_after :]
    out_ref, base = refs[n_pieces], 0
    for ref in refs[:n_pieces]:
        n = ref.shape[0]
        out_ref[base : base + n, :] = ref[...]
        base += n
    if len(refs) > n_pieces + 1:
        refs[-1][...] = out_ref[...].T


def join(pieces, flip, after):
    n_rows = sum(p.shape[0] for p in pieces)
    depth = pieces[0].shape[1]
    tile = depth // 2
    out_specs = [pl.BlockSpec((n_rows, tile), lambda i: (0, i))]
    out_shape = [jax.ShapeDtypeStruct((n_rows, depth), BF16)]
    if flip:
        out_specs.append(pl.BlockSpec((tile, n_rows), lambda i: (i, 0)))
        out_shape.append(jax.ShapeDtypeStruct((depth, n_rows), BF16))
    return pl.pallas_call(
        functools.partial(join_kernel, len(pieces), len(after)),
        grid=(2,),
        in_specs=[pl.BlockSpec((p.shape[0], tile), lambda i: (0, i)) for p in pieces]
        + [pl.BlockSpec(memory_space=pl.ANY)] * len(after),
        out_specs=out_specs,
        out_shape=out_shape,
        compiler_params=pltpu.CompilerParams(vmem_limit_bytes=VMEM_LIMIT),
        cost_estimate=SMALL_COST,
    )(*pieces, *after)


def grads_kernel(own_a, got_a, own_t, got_t, own_g, got_g, flipped, grads, *rest):
    gg_ref, gu_ref, gd_ref, hidden_t, gate_delta, up_delta = rest[-6:]

    @pl.when(pl.program_id(0) == 0)
    def _():
        def total(own, got, i):
            return own[i] + got[i].astype(F32)

        base = 0
        for gate, up, grad_hidden in (
            (
                total(own_t, got_t, 0),
                total(own_t, got_t, 1),
                total(own_g, got_g, own_g.shape[0] - 1),
            ),
            tuple(total(own_a, got_a, i) for i in range(3)),
        ):
            sigmoid_gate = jax.nn.sigmoid(gate)
            activated = gate * sigmoid_gate
            n = gate.shape[0]
            hidden_t[:, base : base + n] = (activated * up).astype(BF16).T
            gate_delta[base : base + n, :] = (
                grad_hidden * up * sigmoid_gate * (1.0 + gate * (1.0 - sigmoid_gate))
            ).astype(BF16)
            up_delta[base : base + n, :] = (grad_hidden * activated).astype(BF16)
            base += n

    gg_ref[...] = jnp.dot(flipped[...], gate_delta[...], preferred_element_type=F32).astype(BF16)
    gu_ref[...] = jnp.dot(flipped[...], up_delta[...], preferred_element_type=F32).astype(BF16)
    gd_ref[...] = jnp.dot(hidden_t[...], grads[...], preferred_element_type=F32).astype(BF16)


def group_grads(
    first, width, a, a_first, t, g, far_first, flipped, grads, hidden_units, so_far, after
):
    depth, n_tokens = flipped.shape
    steps = 4
    tile = depth // steps
    j, far = first // width, far_first // width

    def part(arr, offset):
        return pl.BlockSpec(
            (arr.shape[0], arr.shape[1], width), lambda i: (0, 0, offset // width)
        )

    g_block = pl.BlockSpec((1, g[0].shape[1], width), lambda i: (g[0].shape[0] - 1, 0, far))
    t_block = pl.BlockSpec((2, t[0].shape[1], width), lambda i: (0, 0, far))
    args = [a[0], a[1], t[0], t[1], g[0], g[1], flipped, grads]
    specs = [part(a[0], a_first), part(a[1], a_first), t_block, t_block, g_block, g_block]
    specs += [
        pl.BlockSpec((tile, n_tokens), lambda i: (i, 0)),
        pl.BlockSpec((n_tokens, tile), lambda i: (0, i)),
    ]
    aliases = {}
    if so_far is not None:
        for k, arr in enumerate(so_far):
            aliases[len(args)] = k
            args.append(arr)
            specs.append(pl.BlockSpec(memory_space=pl.ANY))
    for arr in after:
        args.append(arr)
        specs.append(pl.BlockSpec(memory_space=pl.ANY))
    up_shape = jax.ShapeDtypeStruct((depth, hidden_units), BF16)
    down_shape = jax.ShapeDtypeStruct((hidden_units, depth), BF16)
    return pl.pallas_call(
        grads_kernel,
        grid=(steps,),
        in_specs=specs,
        out_specs=[
            pl.BlockSpec((tile, width), lambda i: (i, j)),
            pl.BlockSpec((tile, width), lambda i: (i, j)),
            pl.BlockSpec((width, tile), lambda i: (j, i)),
        ],
        out_shape=[up_shape, up_shape, down_shape],
        scratch_shapes=[
            pltpu.VMEM((width, n_tokens), BF16),
            pltpu.VMEM((n_tokens, width), BF16),
            pltpu.VMEM((n_tokens, width), BF16),
        ],
        input_output_aliases=aliases,
        compiler_params=pltpu.CompilerParams(vmem_limit_bytes=VMEM_LIMIT),
        cost_estimate=SMALL_COST,
    )(*args)


def pair_shards(n_feat, tokens, out_grad, gate_weight, up_weight, down_weight):
    hidden_units = gate_weight.shape[1]
    weights = (gate_weight, up_weight)
    wide = 2 * CHUNK
    n_own = tokens.shape[0]
    partial = partial_products

    def swap(x):
        return lax.ppermute(x, "tok", [(0, 1), (1, 0)])

    def sibling(x):
        return lax.ppermute(x, "feat", [(i, i ^ 1) for i in range(n_feat)])

    def gather(x):
        return [
            lax.ppermute(x, "feat", [(i, (i + k) % n_feat) for i in range(n_feat)])
            for k in range(2, n_feat, 2)
        ]

    near_tokens = [tokens, sibling(tokens)]
    near_grad = [out_grad, sibling(out_grad)]
    token_blocks, grad_blocks = gather(tokens), gather(out_grad)
    near = (n_own, n_own)
    far = ((n_feat // 2 - 1) * n_own,) * 2

    def near_part(first, width, after):
        own, send = partial(
            near_tokens, near_grad, near, weights, down_weight, first, width, after
        )
        return own, swap(send)

    def far_part(first, width, kinds, after):
        own, send = partial(
            far_tokens if "t" in kinds else None,
            far_grad if "g" in kinds else None,
            far,
            weights if "t" in kinds else (),
            down_weight if "g" in kinds else None,
            first, width, after,
        )
        return own, swap(send)

    def far_rows(blocks, after):
        mine = join(blocks, False, after)[0]
        return [mine, sibling(mine)]

    a0 = near_part(0, wide, ())
    a1 = near_part(wide, hidden_units - wide, (a0[0],))
    far_tokens = far_rows(token_blocks, (a1[0], a0[1]))
    t01 = far_part(0, 2 * wide, "t", (a1[1],))
    flipped = join(far_tokens + near_tokens, True, (t01[0],))[1]
    far_grad = far_rows(grad_blocks, (t01[0],))
    g01 = far_part(0, 2 * wide, "g", (t01[0],))
    all_grad = join(far_grad + near_grad, False, (g01[0],))[0]
    f2 = far_part(2 * wide, wide, "tg", (g01[0], t01[1]))
    f3 = far_part(3 * wide, hidden_units - 3 * wide, "tg", (f2[0], g01[1]))

    outs = None
    for first, width, a, a_first, t, g, after in (
        (0, wide, a0, 0, t01, g01, (f3[0],)),
        (wide, wide, a1, 0, t01, g01, ()),
        (2 * wide, wide, a1, wide, f2, f2, ()),
        (3 * wide, hidden_units - 3 * wide, a1, 2 * wide, f3, f3, ()),
    ):
        far_first = wide if first == wide else 0
        outs = group_grads(
            first, width, a, a_first, t, g, far_first, flipped, all_grad, hidden_units,
            outs, after,
        )
    return tuple(outs)


def solution(mesh):
    n_feat, n_tok = mesh.shape["feat"], mesh.shape["tok"]
    pair = n_tok == 2 and n_feat % 2 == 0 and 2 < n_feat <= 8
    return jax.shard_map(
        functools.partial(pair_shards, n_feat) if pair else plain_shards,
        mesh=mesh,
        in_specs=(
            P(("groups", "feat"), "tok"),
            P(("groups", "feat"), "tok"),
            P("tok", "feat"),
            P("tok", "feat"),
            P("feat", "tok"),
        ),
        out_specs=(
            P(("groups", "tok"), "feat"),
            P(("groups", "tok"), "feat"),
            P(("groups", "feat"), "tok"),
        ),
        check_vma=False,
    )
```
